256 devices in a mesh: train: 64 (over z_hi, x, y), layer: 2 (over core), query: 2 (over z_lo).
Axes of the slice: x: 4, y: 4, z: 8 (z_hi: 4, z_lo: 2; z = z_hi * 2 + z_lo), core: 2. Of those that a mesh axis runs over, the one named last changes fastest.
Arguments:
- queries: bfloat16 [2, 512, 2, 16384], P('query', 'train', 'layer'), may hold values from -8 to 8
- train_feats: bfloat16 [24576, 2, 16384], P('train', 'layer'), may hold values from -6 to 6
- train_weight: float32 [24576], P('train'), may hold values from 0.25 to 1
Outputs:
- scores: bfloat16 [2, 512, 24576], P('query', None, 'train')
The draws below stay inside these ranges and needn't reach their ends.
All inputs are finite; a program needn't handle non-finite values.
Results may differ from the reference program's by a relative error of at most 0.001.
Values may be sent and summed in bfloat16 or wider, within the bound.
No kernel may reach another device: no remote copies, remote signals or barrier semaphores. Data moves between devices by JAX's collectives and lax.ppermute only.
A program may use at most 128 MiB of HBM per device.

```python
import math
import jax
import jax.numpy as jnp
from jax import lax

PROJ = 16384
LAYERS = 2
QSETS = 2
QRY_DEV = 512
TRAIN = 24576


def draw_queries(key, part):
    key = jax.random.fold_in(key, 7)
    first, second, third = jax.random.split(key, 3)
    row_scale = jnp.exp(jax.random.uniform(first, (QSETS, QRY_DEV, 1, 1), jnp.float32) * math.log(10.0))
    col_scale = jnp.exp(jax.random.uniform(second, (1, 1, LAYERS, PROJ), jnp.float32) * math.log(10.0))
    base = jnp.clip(jax.random.normal(third, (QSETS, QRY_DEV, LAYERS, PROJ), jnp.float32), -4.0, 4.0)
    return (0.02 * base * row_scale * col_scale).astype(jnp.bfloat16)


def shard_levels(own_key, shape, pieces, smallest, largest):
    factor_of = 1.0
    for axis_at, shards_of in pieces:
        steps = jax.random.uniform(jax.random.fold_in(jax.random.fold_in(own_key, 6), axis_at), (shards_of,), jnp.float32, smallest / len(pieces), largest / len(pieces))
        factor_of = factor_of * jnp.repeat(jnp.exp(steps), shape[axis_at] // shards_of).reshape((-1,) + (1,) * (len(shape) - 1 - axis_at))
    return factor_of


def centred(own_key, dims, width, reach, pieces=(), held_as=jnp.bfloat16):
    result = jax.random.normal(own_key, dims, jnp.float32) * width
    if len(pieces) > 0:
        result = shard_levels(own_key, dims, pieces, -0.22, 0.18) * result
    return jnp.clip(result, min=-reach, max=reach).astype(held_as)


def setup_inputs(seed: int = 0) -> dict:
    splits = jax.random.split(jax.random.key(seed), 4)
    queries = draw_queries(jax.random.fold_in(splits[3], 71), 0)
    train_feats = centred(splits[1], (TRAIN, LAYERS, PROJ), 1.0, 6.0, ((0, 64), (1, 2)))
    train_weight = jnp.clip(jnp.exp(math.log(1.0) - 1.3862944 * jax.random.uniform(splits[2], (TRAIN,), jnp.float32) ** shard_levels(splits[2], (TRAIN,), ((0, 64),), -0.2, 0.2)), 0.25, 1.0)
    return dict(queries=queries, train_feats=train_feats, train_weight=train_weight)


def reference(queries, train_feats, train_weight):
    flat_query = queries.reshape(queries.shape[0] * queries.shape[1], -1)
    flat_train = train_feats.reshape(train_feats.shape[0], -1)
    wide_query = flat_query.astype(jnp.float32)
    norms = lax.optimization_barrier(jnp.sum(wide_query * wide_query, axis=1))
    raw = lax.dot_general(flat_query, flat_train, (((1,), (1,)), ((), ())), preferred_element_type=jnp.float32)
    scaled = raw * train_weight[None, :] * lax.rsqrt(norms + 1e-06)[:, None]
    return scaled.reshape(queries.shape[0], queries.shape[1], -1).astype(jnp.bfloat16)
```

```python
import jax
import jax.numpy as jnp
from jax import lax
from jax.experimental import pallas as pl
from jax.experimental.pallas import tpu as pltpu
from jax.sharding import Mesh, PartitionSpec as P

RING = 4
Z_AXES = ("zh", "query")


def shift(v, axis, by):
    size = lax.axis_size(axis)
    return lax.ppermute(v, axis, [(i, (i + by) % size) for i in range(size)])


def row_product(left, right):
    return lax.dot_general(
        left, right, (((1,), (1,)), ((), ())), preferred_element_type=jnp.float32
    )


def z_planes(own):
    half = own.shape[-1] // 2
    up, down = shift(own, Z_AXES, 1), shift(own, Z_AXES, -1)
    up, down = shift(up, Z_AXES, 1), shift(down, Z_AXES, -1)
    far_up, far_down = shift(up[..., :half], Z_AXES, 1), shift(down[..., half:], Z_AXES, -1)
    far_up, far_down = shift(far_up, Z_AXES, 1), shift(far_down, Z_AXES, -1)
    return own, up, down, far_up, far_down


def ring(v, axis):
    n = v.shape[0] // 2
    left, right = shift(v, axis, 1), shift(v, axis, -1)
    return v, left, right, shift(left[:n], axis, 1), shift(right[n:], axis, -1)


def block_sums(parts, store):
    products, squares = [], []
    for part in parts:
        rows = part.reshape(-1, part.shape[-1])
        wide = rows.astype(jnp.float32)
        products.append(row_product(rows, store))
        squares.append(jnp.sum(wide * wide, axis=1))
    return jnp.concatenate(products, 0), jnp.concatenate(squares, 0)


def finish_kernel(order, mine, other, scale, weight, out):
    def body(i, carry):
        halves = []
        for j in range(2):
            at = pl.multiple_of(order[2 * i + j] * 8, 8)
            rows = pl.ds(at, 8)
            halves.append((mine[rows, :] + other[rows, :]) * weight[...] * scale[rows, :])
        out[pl.ds(pl.multiple_of(i * 16, 16), 16), :] = jnp.concatenate(halves, 0).astype(out.dtype)
        return carry

    lax.fori_loop(0, out.shape[0] // 16, body, 0, unroll=4)


def absolute_order(zh, x, y):
    place = jnp.array([0, 2, 3, 1], jnp.int32)
    r = jnp.arange(RING, dtype=jnp.int32)
    pz, px, py = (place[(r - a) % RING] for a in (zh, x, y))
    return (py[None, None, :] * 16 + px[None, :, None] * 4 + pz[:, None, None]).reshape(-1)


def per_device(queries, train_feats, train_weight):
    own = queries[0, :, 0, :][None]
    store = train_feats[:, 0, :]
    half = own.shape[-1] // 2
    z = z_planes(own)
    planes = jnp.concatenate([z[0], z[1], z[2], jnp.concatenate([z[3], z[4]], -1)], 0)
    first = jnp.concatenate(ring(planes[..., :half], "x"), 0)
    second = jnp.concatenate(ring(planes[..., half:], "y"), 0)
    a_raw, a_norm = block_sums(ring(first, "y"), store[:, :half])
    b_raw, b_norm = block_sums(ring(second, "x"), store[:, half:])
    n_store = store.shape[0]
    flip = lambda v: jnp.swapaxes(v.reshape((4, 4, 32) + v.shape[1:]), 0, 1).reshape(v.shape)
    mine = a_raw + flip(b_raw)
    norm = a_norm + flip(b_norm)
    other = shift(mine, "layer", 1)
    norm = norm + shift(norm, "layer", 1)
    scale = lax.rsqrt(norm + 1e-06)[:, None]
    order = absolute_order(*(lax.axis_index(a) for a in ("zh", "x", "y")))
    vmem = pl.BlockSpec(memory_space=pltpu.VMEM)
    result = pl.pallas_call(
        finish_kernel,
        out_shape=jax.ShapeDtypeStruct((mine.shape[0], n_store), jnp.bfloat16),
        in_specs=[pl.BlockSpec(memory_space=pltpu.SMEM)] + [vmem] * 4,
        out_specs=vmem,
        compiler_params=pltpu.CompilerParams(vmem_limit_bytes=16 * 1024 * 1024),
    )(order, mine, other, scale, train_weight[None, :])
    return result[None, :, :]


def solution(mesh):
    fine = Mesh(
        mesh.devices.reshape(RING, RING, RING, mesh.shape["layer"], mesh.shape["query"]),
        ("zh", "x", "y", "layer", "query"),
    )
    train = ("zh", "x", "y")
    return jax.shard_map(
        per_device,
        mesh=fine,
        in_specs=(P("query", train, "layer", None), P(train, "layer", None), P(train)),
        out_specs=P("query", None, train),
        check_vma=False,
    )
```

```python
import functools

import jax
import jax.numpy as jnp
from jax import lax
from jax.experimental import pallas as pl
from jax.experimental.pallas import tpu as pltpu
from jax.sharding import Mesh, PartitionSpec as P

RING = 4
LANES = 128
DEPTH = 1024
Z_AXES = ("zh", "query")


def shift(v, axis, by):
    size = lax.axis_size(axis)
    return lax.ppermute(v, axis, [(i, (i + by) % size) for i in range(size)])


def row_product(left, right):
    return lax.dot_general(
        left, right, (((1,), (1,)), ((), ())), preferred_element_type=jnp.float32
    )


def z_planes(own):
    half = own.shape[-1] // 2
    up, down = shift(own, Z_AXES, 1), shift(own, Z_AXES, -1)
    up, down = shift(up, Z_AXES, 1), shift(down, Z_AXES, -1)
    far_up, far_down = shift(up[..., :half], Z_AXES, 1), shift(down[..., half:], Z_AXES, -1)
    far_up, far_down = shift(far_up, Z_AXES, 1), shift(far_down, Z_AXES, -1)
    return own, up, down, far_up, far_down


def ring(v, axis):
    n = v.shape[0] // 2
    left, right = shift(v, axis, 1), shift(v, axis, -1)
    return v, left, right, shift(left[:n], axis, 1), shift(right[n:], axis, -1)


def add_kernel(offsets, n_parts, first, *refs):
    count = len(offsets) * n_parts
    a_refs, b_refs = refs[:count], refs[count : 2 * count]
    a_store, b_store = refs[2 * count : 2 * count + 2]
    out = refs[-1]
    n_out = a_store.shape[0]

    @pl.when(pl.program_id(0) == 0)
    def _():
        if first:
            out[...] = jnp.zeros_like(out)
        else:
            out[...] = refs[2 * count + 2][...]

    def terms(parts, store):
        rows = jnp.concatenate([p[...] for p in parts], 0)
        product = row_product(rows, store[...])
        squares = jnp.zeros((rows.shape[0], LANES), jnp.float32)
        for i in range(0, rows.shape[1], LANES):
            wide = rows[:, i : i + LANES].astype(jnp.float32)
            squares += wide * wide
        return product, squares

    a_product, a_squares = terms(a_refs, a_store)
    b_product, b_squares = terms(b_refs, b_store)
    block = a_product.shape[0] // len(offsets)
    strip = block // RING
    for i, offset in enumerate(offsets):
        rows, source = pl.ds(offset * block, block), slice(i * block, (i + 1) * block)
        out[rows, :n_out] += a_product[source]
        out[rows, n_out:] += a_squares[source]
        for j in range(RING):
            rows = pl.ds(j * block + offset * strip, strip)
            source = slice(i * block + j * strip, i * block + (j + 1) * strip)
            out[rows, :n_out] += b_product[source]
            out[rows, n_out:] += b_squares[source]


def add_blocks(sums, offsets, a_parts, b_parts, store):
    n_out = store.shape[0]
    flat = lambda v: v.reshape(-1, v.shape[-1])
    a_parts, b_parts = [flat(v) for v in a_parts], [flat(v) for v in b_parts]
    steps = a_parts[0].shape[1] // DEPTH
    n_rows = sum(v.shape[0] for v in a_parts)
    shape = (RING * n_rows // len(offsets), n_out + LANES)
    part_specs = [pl.BlockSpec((v.shape[0], DEPTH), lambda k: (0, k)) for v in a_parts + b_parts]
    store_specs = [
        pl.BlockSpec((n_out, DEPTH), lambda k: (0, k)),
        pl.BlockSpec((n_out, DEPTH), lambda k: (0, k + steps)),
    ]
    whole = pl.BlockSpec(shape, lambda k: (0, 0))
    earlier = [] if sums is None else [sums]
    return pl.pallas_call(
        functools.partial(
            add_kernel, offsets, len(a_parts) // len(offsets), sums is None
        ),
        grid=(steps,),
        out_shape=jax.ShapeDtypeStruct(shape, jnp.float32),
        in_specs=part_specs + store_specs + [whole] * len(earlier),
        out_specs=whole,
        compiler_params=pltpu.CompilerParams(vmem_limit_bytes=24 * 1024 * 1024),
        cost_estimate=pl.CostEstimate(
            flops=4 * n_rows * steps * DEPTH * n_out,
            bytes_accessed=2 * steps * DEPTH * (2 * n_out + 2 * n_rows),
            transcendentals=0,
        ),
    )(*a_parts, *b_parts, store, store, *earlier)


def finish_kernel(order, mine, other, weight, out):
    n_out = out.shape[1]

    def body(i, carry):
        halves = []
        for j in range(2):
            rows = pl.ds(pl.multiple_of(order[2 * i + j] * 8, 8), 8)
            both = mine[rows, :] + other[rows, :]
            norm = jnp.sum(both[:, n_out:], axis=1, keepdims=True)
            halves.append(both[:, :n_out] * weight[...] * lax.rsqrt(norm + 1e-06))
        out[pl.ds(pl.multiple_of(i * 16, 16), 16), :] = jnp.concatenate(halves, 0).astype(out.dtype)
        return carry

    lax.fori_loop(0, out.shape[0] // 16, body, 0, unroll=4)


def absolute_order(zh, x, y):
    r = jnp.arange(RING, dtype=jnp.int32)

    def place(at):
        off = (r - at) % RING
        return jnp.where(off == 0, 0, jnp.where(off == 3, 1, off + 1))

    pz, px, py = place(zh), place(x), place(y)
    return (py[None, None, :] * 16 + px[None, :, None] * 4 + pz[:, None, None]).reshape(-1)


def per_device(queries, train_feats, train_weight):
    own = queries[0, :, 0, :][None]
    store = train_feats[:, 0, :]
    half = own.shape[-1] // 2
    z = z_planes(own)
    planes = jnp.concatenate([z[0], z[1], z[2], jnp.concatenate([z[3], z[4]], -1)], 0)
    first = jnp.concatenate(ring(planes[..., :half], "x"), 0)
    second = jnp.concatenate(ring(planes[..., half:], "y"), 0)
    a, b = ring(first, "y"), ring(second, "x")
    sums = add_blocks(None, (0,), a[:1], b[:1], store)
    sums = add_blocks(sums, (1, 2), a[1:3], b[1:3], store)
    sums = add_blocks(sums, (3,), a[3:], b[3:], store)
    other = shift(sums, "layer", 1)
    order = absolute_order(*(lax.axis_index(n) for n in ("zh", "x", "y")))
    vmem = pl.BlockSpec(memory_space=pltpu.VMEM)
    result = pl.pallas_call(
        finish_kernel,
        out_shape=jax.ShapeDtypeStruct((sums.shape[0], store.shape[0]), jnp.bfloat16),
        in_specs=[pl.BlockSpec(memory_space=pltpu.SMEM)] + [vmem] * 3,
        out_specs=vmem,
        compiler_params=pltpu.CompilerParams(vmem_limit_bytes=16 * 1024 * 1024),
    )(order, sums, other, train_weight[None, :])
    return result[None, :, :]


def solution(mesh):
    fine = Mesh(
        mesh.devices.reshape(RING, RING, RING, mesh.shape["layer"], mesh.shape["query"]),
        ("zh", "x", "y", "layer", "query"),
    )
    train = ("zh", "x", "y")
    return jax.shard_map(
        per_device,
        mesh=fine,
        in_specs=(P("query", train, "layer", None), P(train, "layer", None), P(train)),
        out_specs=P("query", None, train),
        check_vma=False,
    )
```

```python
import functools

import jax
import jax.numpy as jnp
from jax import lax
from jax.experimental import pallas as pl
from jax.experimental.pallas import tpu as pltpu
from jax.sharding import Mesh, PartitionSpec as P

RING = 4
LANES = 128
Z_AXES = ("zh", "query")


def shift(v, axis, by):
    size = lax.axis_size(axis)
    return lax.ppermute(v, axis, [(i, (i + by) % size) for i in range(size)])


def z_planes(own):
    half = own.shape[-1] // 2
    up, down = shift(own, Z_AXES, 1), shift(own, Z_AXES, -1)
    up, down = shift(up, Z_AXES, 1), shift(down, Z_AXES, -1)
    far_up, far_down = shift(up[..., :half], "zh", 1), shift(down[..., half:], "zh", -1)
    return own, up, down, far_up, far_down


def ring(v, axis):
    n = v.shape[0] // 2
    left, right = shift(v, axis, 1), shift(v, axis, -1)
    return v, left, right, shift(left[:n], axis, 1), shift(right[n:], axis, -1)


def add_kernel(offsets, n_parts, *refs):
    first = offsets == (0,)
    count = len(offsets) * n_parts
    a_refs, b_refs = refs[:count], refs[count : 2 * count]
    stores = refs[2 * count : 2 * count + 2]
    if first:
        out, turned = refs[2 * count + 2], refs[2 * count + 3 :]
        n_out = turned[0].shape[1]
    else:
        out, n_out = refs[-1], stores[0].shape[1]

    @pl.when(pl.program_id(0) == 0)
    def _():
        if first:
            out[...] = jnp.zeros_like(out)
        else:
            out[...] = refs[2 * count + 2][...]

    def terms(which, parts):
        store = stores[which][...]
        if first:
            store = store.T
            turned[which][...] = store
        rows = jnp.concatenate([p[...] for p in parts], 0)
        product = jnp.dot(rows, store, preferred_element_type=jnp.float32)
        squares = jnp.zeros((rows.shape[0], LANES), jnp.float32)
        for i in range(0, rows.shape[1], LANES):
            wide = rows[:, i : i + LANES].astype(jnp.float32)
            squares += wide * wide
        return product, squares

    a_product, a_squares = terms(0, a_refs)
    b_product, b_squares = terms(1, b_refs)
    block = a_product.shape[0] // len(offsets)
    strip = block // RING
    for i, offset in enumerate(offsets):
        rows, source = pl.ds(offset * block, block), slice(i * block, (i + 1) * block)
        out[rows, :n_out] += a_product[source]
        out[rows, n_out:] += a_squares[source]
        for j in range(RING):
            rows = pl.ds(j * block + offset * strip, strip)
            source = slice(i * block + j * strip, i * block + (j + 1) * strip)
            out[rows, :n_out] += b_product[source]
            out[rows, n_out:] += b_squares[source]


def add_blocks(sums, offsets, a_parts, b_parts, stores, n_out, depth):
    flat = lambda v: v.reshape(-1, v.shape[-1])
    a_parts, b_parts = [flat(v) for v in a_parts], [flat(v) for v in b_parts]
    half = a_parts[0].shape[1]
    steps = half // depth
    n_rows = sum(v.shape[0] for v in a_parts)
    shape = (RING * n_rows // len(offsets), n_out + LANES)
    part_specs = [pl.BlockSpec((v.shape[0], depth), lambda k: (0, k)) for v in a_parts + b_parts]
    turned_spec = pl.BlockSpec((depth, n_out), lambda k: (k, 0))
    whole = pl.BlockSpec(shape, lambda k: (0, 0))
    out_shape, out_specs = jax.ShapeDtypeStruct(shape, jnp.float32), whole
    if sums is None:
        store_specs = [
            pl.BlockSpec((n_out, depth), lambda k: (0, k)),
            pl.BlockSpec((n_out, depth), lambda k: (0, k + steps)),
        ]
        turned = jax.ShapeDtypeStruct((half, n_out), stores[0].dtype)
        out_shape, out_specs = (out_shape, turned, turned), (whole, turned_spec, turned_spec)
        earlier = []
    else:
        store_specs = [turned_spec] * 2
        earlier = [sums]
    return pl.pallas_call(
        functools.partial(add_kernel, offsets, len(a_parts) // len(offsets)),
        grid=(steps,),
        out_shape=out_shape,
        in_specs=part_specs + store_specs + [whole] * len(earlier),
        out_specs=out_specs,
        compiler_params=pltpu.CompilerParams(vmem_limit_bytes=26 * 1024 * 1024),
        cost_estimate=pl.CostEstimate(
            flops=4 * n_rows * half * n_out,
            bytes_accessed=4 * half * (n_out + n_rows),
            transcendentals=0,
        ),
    )(*a_parts, *b_parts, *stores, *earlier)


def finish_kernel(order, mine, other, weight, out):
    n_out = out.shape[1]

    def body(i, carry):
        halves = []
        for j in range(2):
            rows = pl.ds(pl.multiple_of(order[2 * i + j] * 8, 8), 8)
            both = mine[rows, :] + other[rows, :]
            norm = jnp.sum(both[:, n_out:], axis=1, keepdims=True)
            halves.append(both[:, :n_out] * weight[...] * lax.rsqrt(norm + 1e-06))
        out[pl.ds(pl.multiple_of(i * 16, 16), 16), :] = jnp.concatenate(halves, 0).astype(out.dtype)
        return carry

    lax.fori_loop(0, out.shape[0] // 16, body, 0, unroll=4)


def absolute_order(zh, x, y):
    r = jnp.arange(RING, dtype=jnp.int32)

    def place(at):
        off = (r - at) % RING
        return jnp.where(off == 0, 0, jnp.where(off == 3, 1, off + 1))

    pz, px, py = place(zh), place(x), place(y)
    return (py[None, None, :] * 16 + px[None, :, None] * 4 + pz[:, None, None]).reshape(-1)


def per_device(queries, train_feats, train_weight):
    own = queries[0, :, 0, :][None]
    store = train_feats[:, 0, :]
    half = own.shape[-1] // 2
    z = z_planes(own)
    a_planes = jnp.concatenate([v[..., :half] for v in z[:3]] + [z[3]], 0)
    b_planes = jnp.concatenate([v[..., half:] for v in z[:3]] + [z[4]], 0)
    first = jnp.concatenate(ring(a_planes, "x"), 0)
    second = jnp.concatenate(ring(b_planes, "y"), 0)
    a, b = ring(first, "y"), ring(second, "x")
    n_out = store.shape[0]
    sums, *turned = add_blocks(None, (0,), a[:1], b[:1], (store, store), n_out, 1024)
    sums = add_blocks(sums, (1, 2), a[1:3], b[1:3], turned, n_out, 2048)
    sums = add_blocks(sums, (3,), a[3:], b[3:], turned, n_out, 4096)
    other = shift(sums, "layer", 1)
    order = absolute_order(*(lax.axis_index(n) for n in ("zh", "x", "y")))
    vmem = pl.BlockSpec(memory_space=pltpu.VMEM)
    result = pl.pallas_call(
        finish_kernel,
        out_shape=jax.ShapeDtypeStruct((sums.shape[0], n_out), jnp.bfloat16),
        in_specs=[pl.BlockSpec(memory_space=pltpu.SMEM)] + [vmem] * 3,
        out_specs=vmem,
        compiler_params=pltpu.CompilerParams(vmem_limit_bytes=16 * 1024 * 1024),
    )(order, sums, other, train_weight[None, :])
    return result[None, :, :]


def solution(mesh):
    fine = Mesh(
        mesh.devices.reshape(RING, RING, RING, mesh.shape["layer"], mesh.shape["query"]),
        ("zh", "x", "y", "layer", "query"),
    )
    train = ("zh", "x", "y")
    return jax.shard_map(
        per_device,
        mesh=fine,
        in_specs=(P("query", train, "layer", None), P(train, "layer", None), P(train)),
        out_specs=P("query", None, train),
        check_vma=False,
    )
```

```python
import functools

import jax
import jax.numpy as jnp
from jax import lax
from jax.experimental import pallas as pl
from jax.experimental.pallas import tpu as pltpu
from jax.sharding import Mesh, PartitionSpec as P

RING = 4
LANES = 128
Z_AXES = ("zh", "query")


def shift(v, axis, by):
    size = lax.axis_size(axis)
    return lax.ppermute(v, axis, [(i, (i + by) % size) for i in range(size)])


def z_planes(a_own, b_own):
    def twice(v, by):
        return shift(shift(v, Z_AXES, by), Z_AXES, by)

    a_up, b_down = twice(a_own, 1), twice(b_own, -1)
    a_far, b_far = shift(a_up, "zh", 1), shift(b_down, "zh", -1)
    return (a_own, a_up, twice(a_own, -1), a_far), (b_own, twice(b_own, 1), b_down, b_far)


def ring(v, axis):
    n = v.shape[0] // 2
    left, right = shift(v, axis, 1), shift(v, axis, -1)
    return v, left, right, shift(left[:n], axis, 1), shift(right[n:], axis, -1)


def add_kernel(offsets, n_parts, *refs):
    first = offsets == (0,)
    count = len(offsets) * n_parts
    a_refs, b_refs = refs[:count], refs[count : 2 * count]
    stores = refs[2 * count : 2 * count + 2]
    if first:
        out, turned = refs[2 * count + 2], refs[2 * count + 3 :]
        n_out = turned[0].shape[1]
    else:
        out, n_out = refs[-1], stores[0].shape[1]

    @pl.when(pl.program_id(0) == 0)
    def _():
        if first:
            out[...] = jnp.zeros_like(out)
        else:
            out[...] = refs[2 * count + 2][...]

    def terms(which, parts):
        store = stores[which][...]
        if first:
            store = store.T
            turned[which][...] = store
        rows = jnp.concatenate([p[...] for p in parts], 0)
        product = jnp.dot(rows, store, preferred_element_type=jnp.float32)
        squares = jnp.zeros((rows.shape[0], LANES), jnp.float32)
        for i in range(0, rows.shape[1], LANES):
            wide = rows[:, i : i + LANES].astype(jnp.float32)
            squares += wide * wide
        return product, squares

    a_product, a_squares = terms(0, a_refs)
    b_product, b_squares = terms(1, b_refs)
    block = a_product.shape[0] // len(offsets)
    strip = block // RING
    for i, offset in enumerate(offsets):
        rows, source = pl.ds(offset * block, block), slice(i * block, (i + 1) * block)
        out[rows, :n_out] += a_product[source]
        out[rows, n_out:] += a_squares[source]
        for j in range(RING):
            rows = pl.ds(j * block + offset * strip, strip)
            source = slice(i * block + j * strip, i * block + (j + 1) * strip)
            out[rows, :n_out] += b_product[source]
            out[rows, n_out:] += b_squares[source]


def add_blocks(sums, offsets, a_parts, b_parts, stores, n_out, depth):
    flat = lambda v: v.reshape(-1, v.shape[-1])
    a_parts, b_parts = [flat(v) for v in a_parts], [flat(v) for v in b_parts]
    half = a_parts[0].shape[1]
    steps = half // depth
    n_rows = sum(v.shape[0] for v in a_parts)
    shape = (RING * n_rows // len(offsets), n_out + LANES)
    part_specs = [pl.BlockSpec((v.shape[0], depth), lambda k: (0, k)) for v in a_parts + b_parts]
    turned_spec = pl.BlockSpec((depth, n_out), lambda k: (k, 0))
    whole = pl.BlockSpec(shape, lambda k: (0, 0))
    out_shape, out_specs = jax.ShapeDtypeStruct(shape, jnp.float32), whole
    if sums is None:
        store_specs = [
            pl.BlockSpec((n_out, depth), lambda k: (0, k)),
            pl.BlockSpec((n_out, depth), lambda k: (0, k + steps)),
        ]
        turned = jax.ShapeDtypeStruct((half, n_out), stores[0].dtype)
        out_shape, out_specs = (out_shape, turned, turned), (whole, turned_spec, turned_spec)
        earlier = []
    else:
        store_specs = [turned_spec] * 2
        earlier = [sums]
    return pl.pallas_call(
        functools.partial(add_kernel, offsets, len(a_parts) // len(offsets)),
        grid=(steps,),
        out_shape=out_shape,
        in_specs=part_specs + store_specs + [whole] * len(earlier),
        out_specs=out_specs,
        compiler_params=pltpu.CompilerParams(vmem_limit_bytes=26 * 1024 * 1024),
        cost_estimate=pl.CostEstimate(
            flops=4 * n_rows * half * n_out,
            bytes_accessed=4 * half * (n_out + n_rows),
            transcendentals=0,
        ),
    )(*a_parts, *b_parts, *stores, *earlier)


def finish_kernel(order, mine, other, weight, out, scaled):
    n_out = out.shape[1]
    for i in range(0, out.shape[0], 64):
        rows = slice(i, i + 64)
        both = mine[rows, :] + other[rows, :]
        norm = jnp.sum(both[:, n_out:], axis=1, keepdims=True)
        scaled[rows, :] = both[:, :n_out] * weight[...] * lax.rsqrt(norm + 1e-06)
    for i in range(0, out.shape[0], 16):
        pair = [scaled[pl.ds(pl.multiple_of(order[i // 8 + j] * 8, 8), 8), :] for j in range(2)]
        out[i : i + 16, :] = jnp.concatenate(pair, 0).astype(out.dtype)


def absolute_order(zh, x, y):
    r = jnp.arange(RING, dtype=jnp.int32)

    def place(at):
        off = (r - at) % RING
        return jnp.where(off == 0, 0, jnp.where(off == 3, 1, off + 1))

    pz, px, py = place(zh), place(x), place(y)
    return (py[None, None, :] * 16 + px[None, :, None] * 4 + pz[:, None, None]).reshape(-1)


def per_device(queries, train_feats, train_weight):
    own = queries[0, :, 0, :][None]
    store = train_feats[:, 0, :]
    half = own.shape[-1] // 2
    a_planes, b_planes = (
        jnp.concatenate(v, 0) for v in z_planes(own[..., :half], own[..., half:])
    )
    first = jnp.concatenate(ring(a_planes, "x"), 0)
    second = jnp.concatenate(ring(b_planes, "y"), 0)
    a, b = ring(first, "y"), ring(second, "x")
    n_out = store.shape[0]
    sums, *turned = add_blocks(None, (0,), a[:1], b[:1], (store, store), n_out, 1024)
    sums = add_blocks(sums, (1, 2), a[1:3], b[1:3], turned, n_out, 2048)
    sums = add_blocks(sums, (3,), a[3:], b[3:], turned, n_out, 4096)
    other = shift(sums, "layer", 1)
    order = absolute_order(*(lax.axis_index(n) for n in ("zh", "x", "y")))
    vmem = pl.BlockSpec(memory_space=pltpu.VMEM)
    result = pl.pallas_call(
        finish_kernel,
        out_shape=jax.ShapeDtypeStruct((sums.shape[0], n_out), jnp.bfloat16),
        in_specs=[pl.BlockSpec(memory_space=pltpu.SMEM)] + [vmem] * 3,
        out_specs=vmem,
        scratch_shapes=[pltpu.VMEM((sums.shape[0], n_out), jnp.float32)],
        compiler_params=pltpu.CompilerParams(vmem_limit_bytes=16 * 1024 * 1024),
    )(order, sums, other, train_weight[None, :])
    return result[None, :, :]


def solution(mesh):
    fine = Mesh(
        mesh.devices.reshape(RING, RING, RING, mesh.shape["layer"], mesh.shape["query"]),
        ("zh", "x", "y", "layer", "query"),
    )
    train = ("zh", "x", "y")
    return jax.shard_map(
        per_device,
        mesh=fine,
        in_specs=(P("query", train, "layer", None), P(train, "layer", None), P(train)),
        out_specs=P("query", None, train),
        check_vma=False,
    )
```

```python
import functools

import jax
import jax.numpy as jnp
from jax import lax
from jax.experimental import pallas as pl
from jax.experimental.pallas import tpu as pltpu
from jax.sharding import Mesh, PartitionSpec as P

RING = 4
LANES = 128
Z_AXES = ("zh", "query")


def shift(v, axis, by):
    size = lax.axis_size(axis)
    return lax.ppermute(v, axis, [(i, (i + by) % size) for i in range(size)])


def z_planes(a_own, b_own):
    def twice(v, by):
        return shift(shift(v, Z_AXES, by), Z_AXES, by)

    a_up, b_down = twice(a_own, 1), twice(b_own, -1)
    a_far, b_far = shift(a_up, "zh", 1), shift(b_down, "zh", -1)
    return (a_own, a_up, twice(a_own, -1), a_far), (b_own, twice(b_own, 1), b_down, b_far)


def ring(v, axis):
    n = v.shape[0] // 2
    left, right = shift(v, axis, 1), shift(v, axis, -1)
    return v, left, right, shift(left[:n], axis, 1), shift(right[n:], axis, -1)


def lane_squares(rows):
    squares = jnp.zeros((rows.shape[0], LANES), jnp.float32)
    for i in range(0, rows.shape[1], LANES):
        wide = rows[:, i : i + LANES].astype(jnp.float32)
        squares += wide * wide
    return squares


def add_rows(out, n_out, offsets, a_terms, b_terms):
    (a_product, a_squares), (b_product, b_squares) = a_terms, b_terms
    block = a_product.shape[0] // len(offsets)
    strip = block // RING
    for i, offset in enumerate(offsets):
        rows, source = pl.ds(offset * block, block), slice(i * block, (i + 1) * block)
        out[rows, :n_out] += a_product[source]
        out[rows, n_out:] += a_squares[source]
        for j in range(RING):
            rows = pl.ds(j * block + offset * strip, strip)
            source = slice(i * block + j * strip, i * block + (j + 1) * strip)
            out[rows, :n_out] += b_product[source]
            out[rows, n_out:] += b_squares[source]


def last_kernel(offset, depth, *refs):
    count = (len(refs) - 4) // 2
    a_refs, b_refs = refs[:count], refs[count : 2 * count]
    a_store, b_store, _, out = refs[2 * count :]
    n_out = a_store.shape[1]

    def terms(parts, store):
        product, squares = 0.0, 0.0
        for k in range(0, store.shape[0], depth):
            rows = jnp.concatenate([p[:, k : k + depth] for p in parts], 0)
            product += jnp.dot(rows, store[k : k + depth, :], preferred_element_type=jnp.float32)
            squares += lane_squares(rows)
        return product, squares

    add_rows(out, n_out, (offset,), terms(a_refs, a_store), terms(b_refs, b_store))


def add_kernel(offsets, n_parts, *refs):
    first = offsets == (0,)
    count = len(offsets) * n_parts
    a_refs, b_refs = refs[:count], refs[count : 2 * count]
    stores = refs[2 * count : 2 * count + 2]
    if first:
        out, turned = refs[2 * count + 2], refs[2 * count + 3 :]
        n_out = turned[0].shape[1]
    else:
        out, n_out = refs[-1], stores[0].shape[1]

    @pl.when(pl.program_id(0) == 0)
    def _():
        if first:
            out[...] = jnp.zeros_like(out)
        else:
            out[...] = refs[2 * count + 2][...]

    def terms(which, parts):
        store = stores[which][...]
        if first:
            store = store.T
            turned[which][...] = store
        rows = jnp.concatenate([p[...] for p in parts], 0)
        return jnp.dot(rows, store, preferred_element_type=jnp.float32), lane_squares(rows)

    add_rows(out, n_out, offsets, terms(0, a_refs), terms(1, b_refs))


def add_blocks(sums, offsets, a_parts, b_parts, stores, n_out, depth):
    flat = lambda v: v.reshape(-1, v.shape[-1])
    a_parts, b_parts = [flat(v) for v in a_parts], [flat(v) for v in b_parts]
    half = a_parts[0].shape[1]
    steps = half // depth
    n_rows = sum(v.shape[0] for v in a_parts)
    shape = (RING * n_rows // len(offsets), n_out + LANES)
    part_specs = [pl.BlockSpec((v.shape[0], depth), lambda k: (0, k)) for v in a_parts + b_parts]
    turned_spec = pl.BlockSpec((depth, n_out), lambda k: (k, 0))
    whole = pl.BlockSpec(shape, lambda k: (0, 0))
    out_shape, out_specs = jax.ShapeDtypeStruct(shape, jnp.float32), whole
    if sums is None:
        store_specs = [
            pl.BlockSpec((n_out, depth), lambda k: (0, k)),
            pl.BlockSpec((n_out, depth), lambda k: (0, k + steps)),
        ]
        turned = jax.ShapeDtypeStruct((half, n_out), stores[0].dtype)
        out_shape, out_specs = (out_shape, turned, turned), (whole, turned_spec, turned_spec)
        earlier = []
    else:
        store_specs = [turned_spec] * 2
        earlier = [sums]
    return pl.pallas_call(
        functools.partial(add_kernel, offsets, len(a_parts) // len(offsets)),
        grid=(steps,),
        out_shape=out_shape,
        in_specs=part_specs + store_specs + [whole] * len(earlier),
        out_specs=out_specs,
        compiler_params=pltpu.CompilerParams(vmem_limit_bytes=26 * 1024 * 1024),
        cost_estimate=pl.CostEstimate(
            flops=4 * n_rows * half * n_out,
            bytes_accessed=4 * half * (n_out + n_rows),
            transcendentals=0,
        ),
    )(*a_parts, *b_parts, *stores, *earlier)


def add_last(sums, offset, a_parts, b_parts, turned, depth):
    flat = lambda v: v.reshape(-1, v.shape[-1])
    operands = [flat(v) for v in (*a_parts, *b_parts)] + [*turned, sums]
    vmem = pl.BlockSpec(memory_space=pltpu.VMEM)
    return pl.pallas_call(
        functools.partial(last_kernel, offset, depth),
        out_shape=jax.ShapeDtypeStruct(sums.shape, sums.dtype),
        in_specs=[vmem] * len(operands),
        out_specs=vmem,
        input_output_aliases={len(operands) - 1: 0},
        compiler_params=pltpu.CompilerParams(vmem_limit_bytes=26 * 1024 * 1024),
    )(*operands)


def finish_kernel(order, mine, other, weight, out, scaled):
    n_out = out.shape[1]
    for i in range(0, out.shape[0], 64):
        rows = slice(i, i + 64)
        both = mine[rows, :] + other[rows, :]
        norm = jnp.sum(both[:, n_out:], axis=1, keepdims=True)
        scaled[rows, :] = both[:, :n_out] * weight[...] * lax.rsqrt(norm + 1e-06)
    for i in range(0, out.shape[0], 16):
        pair = [scaled[pl.ds(pl.multiple_of(order[i // 8 + j] * 8, 8), 8), :] for j in range(2)]
        out[i : i + 16, :] = jnp.concatenate(pair, 0).astype(out.dtype)


def absolute_order(zh, x, y):
    r = jnp.arange(RING, dtype=jnp.int32)

    def place(at):
        off = (r - at) % RING
        return jnp.where(off == 0, 0, jnp.where(off == 3, 1, off + 1))

    pz, px, py = place(zh), place(x), place(y)
    return (py[None, None, :] * 16 + px[None, :, None] * 4 + pz[:, None, None]).reshape(-1)


def per_device(queries, train_feats, train_weight):
    own = queries[0, :, 0, :][None]
    store = train_feats[:, 0, :]
    half = own.shape[-1] // 2
    a_planes, b_planes = (
        jnp.concatenate(v, 0) for v in z_planes(own[..., :half], own[..., half:])
    )
    first = jnp.concatenate(ring(a_planes, "x"), 0)
    second = jnp.concatenate(ring(b_planes, "y"), 0)
    a, b = ring(first, "y"), ring(second, "x")
    n_out = store.shape[0]
    sums, *turned = add_blocks(None, (0,), a[:1], b[:1], (store, store), n_out, 1024)
    sums = add_blocks(sums, (1, 2), a[1:3], b[1:3], turned, n_out, 2048)
    sums = add_last(sums, 3, a[3:], b[3:], turned, 2048)
    other = shift(sums, "layer", 1)
    order = absolute_order(*(lax.axis_index(n) for n in ("zh", "x", "y")))
    vmem = pl.BlockSpec(memory_space=pltpu.VMEM)
    result = pl.pallas_call(
        finish_kernel,
        out_shape=jax.ShapeDtypeStruct((sums.shape[0], n_out), jnp.bfloat16),
        in_specs=[pl.BlockSpec(memory_space=pltpu.SMEM)] + [vmem] * 3,
        out_specs=vmem,
        scratch_shapes=[pltpu.VMEM((sums.shape[0], n_out), jnp.float32)],
        compiler_params=pltpu.CompilerParams(vmem_limit_bytes=16 * 1024 * 1024),
    )(order, sums, other, train_weight[None, :])
    return result[None, :, :]


def solution(mesh):
    fine = Mesh(
        mesh.devices.reshape(RING, RING, RING, mesh.shape["layer"], mesh.shape["query"]),
        ("zh", "x", "y", "layer", "query"),
    )
    train = ("zh", "x", "y")
    return jax.shard_map(
        per_device,
        mesh=fine,
        in_specs=(P("query", train, "layer", None), P(train, "layer", None), P(train)),
        out_specs=P("query", None, train),
        check_vma=False,
    )
```

```python
import functools

import jax
import jax.numpy as jnp
from jax import lax
from jax.experimental import pallas as pl
from jax.experimental.pallas import tpu as pltpu
from jax.sharding import Mesh, PartitionSpec as P

RING = 4
LANES = 128
Z_AXES = ("zh", "query")


def shift(v, axis, by):
    size = lax.axis_size(axis)
    return lax.ppermute(v, axis, [(i, (i + by) % size) for i in range(size)])


def z_planes(a_own, b_own):
    def twice(v, by):
        return shift(shift(v, Z_AXES, by), Z_AXES, by)

    a_up, b_down = twice(a_own, 1), twice(b_own, -1)
    a_far, b_far = shift(a_up, "zh", 1), shift(b_down, "zh", -1)
    return (a_own, a_up, twice(a_own, -1), a_far), (b_own, twice(b_own, 1), b_down, b_far)


def ring(v, axis):
    n = v.shape[0] // 2
    left, right = shift(v, axis, 1), shift(v, axis, -1)
    return v, left, right, shift(left[:n], axis, 1), shift(right[n:], axis, -1)


def lane_squares(rows):
    squares = jnp.zeros((rows.shape[0], LANES), jnp.float32)
    for i in range(0, rows.shape[1], LANES):
        wide = rows[:, i : i + LANES].astype(jnp.float32)
        squares += wide * wide
    return squares


def add_rows(out, n_out, offsets, a_terms, b_terms):
    (a_product, a_squares), (b_product, b_squares) = a_terms, b_terms
    block = a_product.shape[0] // len(offsets)
    strip = block // RING
    for i, offset in enumerate(offsets):
        rows, source = pl.ds(offset * block, block), slice(i * block, (i + 1) * block)
        out[rows, :n_out] += a_product[source]
        out[rows, n_out:] += a_squares[source]
        for j in range(RING):
            rows = pl.ds(j * block + offset * strip, strip)
            source = slice(i * block + j * strip, i * block + (j + 1) * strip)
            out[rows, :n_out] += b_product[source]
            out[rows, n_out:] += b_squares[source]


def last_kernel(offset, depth, *refs):
    count = (len(refs) - 4) // 2
    a_refs, b_refs = refs[:count], refs[count : 2 * count]
    a_store, b_store, _, out = refs[2 * count :]
    n_out = a_store.shape[1]

    def terms(parts, store):
        product, squares = 0.0, 0.0
        for k in range(0, store.shape[0], depth):
            rows = jnp.concatenate([p[:, k : k + depth] for p in parts], 0)
            product += jnp.dot(rows, store[k : k + depth, :], preferred_element_type=jnp.float32)
            squares += lane_squares(rows)
        return product, squares

    add_rows(out, n_out, (offset,), terms(a_refs, a_store), terms(b_refs, b_store))


def add_kernel(offsets, n_parts, *refs):
    first = offsets == (0,)
    count = len(offsets) * n_parts
    a_refs, b_refs = refs[:count], refs[count : 2 * count]
    stores = refs[2 * count : 2 * count + 2]
    if first:
        out, turned = refs[2 * count + 2], refs[2 * count + 3 :]
        n_out = turned[0].shape[1]
    else:
        out, n_out = refs[-1], stores[0].shape[1]

    @pl.when(pl.program_id(0) == 0)
    def _():
        if first:
            out[...] = jnp.zeros_like(out)
        else:
            out[...] = refs[2 * count + 2][...]

    def terms(which, parts):
        store = stores[which][...]
        if first:
            store = store.T
            turned[which][...] = store
        rows = jnp.concatenate([p[...] for p in parts], 0)
        return jnp.dot(rows, store, preferred_element_type=jnp.float32), lane_squares(rows)

    add_rows(out, n_out, offsets, terms(0, a_refs), terms(1, b_refs))


def add_blocks(sums, offsets, a_parts, b_parts, stores, n_out, depth):
    flat = lambda v: v.reshape(-1, v.shape[-1])
    a_parts, b_parts = [flat(v) for v in a_parts], [flat(v) for v in b_parts]
    half = a_parts[0].shape[1]
    steps = half // depth
    n_rows = sum(v.shape[0] for v in a_parts)
    shape = (RING * n_rows // len(offsets), n_out + LANES)
    part_specs = [pl.BlockSpec((v.shape[0], depth), lambda k: (0, k)) for v in a_parts + b_parts]
    turned_spec = pl.BlockSpec((depth, n_out), lambda k: (k, 0))
    whole = pl.BlockSpec(shape, lambda k: (0, 0))
    out_shape, out_specs = jax.ShapeDtypeStruct(shape, jnp.float32), whole
    if sums is None:
        store_specs = [
            pl.BlockSpec((n_out, depth), lambda k: (0, k)),
            pl.BlockSpec((n_out, depth), lambda k: (0, k + steps)),
        ]
        turned = jax.ShapeDtypeStruct((half, n_out), stores[0].dtype)
        out_shape, out_specs = (out_shape, turned, turned), (whole, turned_spec, turned_spec)
        earlier = []
    else:
        store_specs = [turned_spec] * 2
        earlier = [sums]
    return pl.pallas_call(
        functools.partial(add_kernel, offsets, len(a_parts) // len(offsets)),
        grid=(steps,),
        out_shape=out_shape,
        in_specs=part_specs + store_specs + [whole] * len(earlier),
        out_specs=out_specs,
        compiler_params=pltpu.CompilerParams(vmem_limit_bytes=26 * 1024 * 1024),
        cost_estimate=pl.CostEstimate(
            flops=4 * n_rows * half * n_out,
            bytes_accessed=4 * half * (n_out + n_rows),
            transcendentals=0,
        ),
    )(*a_parts, *b_parts, *stores, *earlier)


def add_last(sums, offset, a_parts, b_parts, turned, depth):
    flat = lambda v: v.reshape(-1, v.shape[-1])
    operands = [flat(v) for v in (*a_parts, *b_parts)] + [*turned, sums]
    vmem = pl.BlockSpec(memory_space=pltpu.VMEM)
    return pl.pallas_call(
        functools.partial(last_kernel, offset, depth),
        out_shape=jax.ShapeDtypeStruct(sums.shape, sums.dtype),
        in_specs=[vmem] * len(operands),
        out_specs=vmem,
        input_output_aliases={len(operands) - 1: 0},
        compiler_params=pltpu.CompilerParams(vmem_limit_bytes=26 * 1024 * 1024),
    )(*operands)


def finish_kernel(order, mine, other, weight, out, scaled):
    n_out = out.shape[1]
    for i in range(0, out.shape[0], 64):
        rows = slice(i, i + 64)
        both = mine[rows, :] + other[rows, :]
        norm = jnp.sum(both[:, n_out:], axis=1, keepdims=True)
        scaled[rows, :] = both[:, :n_out] * weight[...] * lax.rsqrt(norm + 1e-06)
    for i in range(0, out.shape[0], 16):
        pair = [scaled[pl.ds(pl.multiple_of(order[i // 8 + j] * 8, 8), 8), :] for j in range(2)]
        out[i : i + 16, :] = jnp.concatenate(pair, 0).astype(out.dtype)


def absolute_order(zh, x, y):
    r = jnp.arange(RING, dtype=jnp.int32)

    def place(at):
        off = (r - at) % RING
        return jnp.where(off == 0, 0, jnp.where(off == 3, 1, off + 1))

    pz, px, py = place(zh), place(x), place(y)
    return (py[None, None, :] * 16 + px[None, :, None] * 4 + pz[:, None, None]).reshape(-1)


def per_device(queries, train_feats, train_weight):
    own = queries[0, :, 0, :][None]
    store = train_feats[:, 0, :]
    half = own.shape[-1] // 2
    a_planes, b_planes = (
        jnp.concatenate(v, 0) for v in z_planes(own[..., :half], own[..., half:])
    )
    first = jnp.concatenate(ring(a_planes, "x"), 0)
    second = jnp.concatenate(ring(b_planes, "y"), 0)
    a, b = ring(first, "y"), ring(second, "x")
    n_out = store.shape[0]
    sums, *turned = add_blocks(None, (0,), a[:1], b[:1], (store, store), n_out, 2048)
    sums = add_blocks(sums, (1, 2), a[1:3], b[1:3], turned, n_out, 2048)
    sums = add_last(sums, 3, a[3:], b[3:], turned, 2048)
    other = shift(sums, "layer", 1)
    order = absolute_order(*(lax.axis_index(n) for n in ("zh", "x", "y")))
    vmem = pl.BlockSpec(memory_space=pltpu.VMEM)
    result = pl.pallas_call(
        finish_kernel,
        out_shape=jax.ShapeDtypeStruct((sums.shape[0], n_out), jnp.bfloat16),
        in_specs=[pl.BlockSpec(memory_space=pltpu.SMEM)] + [vmem] * 3,
        out_specs=vmem,
        scratch_shapes=[pltpu.VMEM((sums.shape[0], n_out), jnp.float32)],
        compiler_params=pltpu.CompilerParams(vmem_limit_bytes=16 * 1024 * 1024),
    )(order, sums, other, train_weight[None, :])
    return result[None, :, :]


def solution(mesh):
    fine = Mesh(
        mesh.devices.reshape(RING, RING, RING, mesh.shape["layer"], mesh.shape["query"]),
        ("zh", "x", "y", "layer", "query"),
    )
    train = ("zh", "x", "y")
    return jax.shard_map(
        per_device,
        mesh=fine,
        in_specs=(P("query", train, "layer", None), P(train, "layer", None), P(train)),
        out_specs=P("query", None, train),
        check_vma=False,
    )
```

```python
import functools

import jax
import jax.numpy as jnp
from jax import lax
from jax.experimental import pallas as pl
from jax.experimental.pallas import tpu as pltpu
from jax.sharding import Mesh, PartitionSpec as P

RING = 4
LANES = 128
Z_AXES = ("zh", "query")


def shift(v, axis, by):
    size = lax.axis_size(axis)
    return lax.ppermute(v, axis, [(i, (i + by) % size) for i in range(size)])


def z_planes(a_own, b_own):
    def twice(v, by):
        return shift(shift(v, Z_AXES, by), Z_AXES, by)

    a_up, b_down = twice(a_own, 1), twice(b_own, -1)
    a_far, b_far = shift(a_up, "zh", 1), shift(b_down, "zh", -1)
    return (a_own, a_up, twice(a_own, -1), a_far), (b_own, twice(b_own, 1), b_down, b_far)


def ring(v, axis):
    n = v.shape[0] // 2
    left, right = shift(v, axis, 1), shift(v, axis, -1)
    return v, left, right, shift(left[:n], axis, 1), shift(right[n:], axis, -1)


def lane_squares(rows):
    squares = jnp.zeros((rows.shape[0], LANES), jnp.float32)
    for i in range(0, rows.shape[1], LANES):
        wide = rows[:, i : i + LANES].astype(jnp.float32)
        squares += wide * wide
    return squares


def add_rows(out, n_out, offsets, a_terms, b_terms):
    (a_product, a_squares), (b_product, b_squares) = a_terms, b_terms
    block = a_product.shape[0] // len(offsets)
    strip = block // RING
    for i, offset in enumerate(offsets):
        rows, source = pl.ds(offset * block, block), slice(i * block, (i + 1) * block)
        out[rows, :n_out] += a_product[source]
        out[rows, n_out:] += a_squares[source]
        for j in range(RING):
            rows = pl.ds(j * block + offset * strip, strip)
            source = slice(i * block + j * strip, i * block + (j + 1) * strip)
            out[rows, :n_out] += b_product[source]
            out[rows, n_out:] += b_squares[source]


def last_kernel(offset, depth, *refs):
    count = (len(refs) - 4) // 2
    a_refs, b_refs = refs[:count], refs[count : 2 * count]
    a_store, b_store, _, out = refs[2 * count :]
    n_out = a_store.shape[1]

    def terms(parts, store):
        product, squares = 0.0, 0.0
        for k in range(0, store.shape[0], depth):
            rows = jnp.concatenate([p[:, k : k + depth] for p in parts], 0)
            product += jnp.dot(rows, store[k : k + depth, :], preferred_element_type=jnp.float32)
            squares += lane_squares(rows)
        return product, squares

    add_rows(out, n_out, (offset,), terms(a_refs, a_store), terms(b_refs, b_store))


def add_kernel(offsets, n_parts, *refs):
    first = offsets == (0,)
    count = len(offsets) * n_parts
    a_refs, b_refs = refs[:count], refs[count : 2 * count]
    stores = refs[2 * count : 2 * count + 2]
    if first:
        out, turned = refs[2 * count + 2], refs[2 * count + 3 :]
        n_out = turned[0].shape[1]
    else:
        out, n_out = refs[-1], stores[0].shape[1]

    @pl.when(pl.program_id(0) == 0)
    def _():
        if first:
            out[...] = jnp.zeros_like(out)
        else:
            out[...] = refs[2 * count + 2][...]

    def terms(which, parts):
        store = stores[which][...]
        if first:
            store = store.T
            turned[which][...] = store
        rows = jnp.concatenate([p[...] for p in parts], 0)
        return jnp.dot(rows, store, preferred_element_type=jnp.float32), lane_squares(rows)

    add_rows(out, n_out, offsets, terms(0, a_refs), terms(1, b_refs))


def add_blocks(sums, offsets, a_parts, b_parts, stores, n_out, depth):
    flat = lambda v: v.reshape(-1, v.shape[-1])
    a_parts, b_parts = [flat(v) for v in a_parts], [flat(v) for v in b_parts]
    half = a_parts[0].shape[1]
    steps = half // depth
    n_rows = sum(v.shape[0] for v in a_parts)
    shape = (RING * n_rows // len(offsets), n_out + LANES)
    part_specs = [pl.BlockSpec((v.shape[0], depth), lambda k: (0, k)) for v in a_parts + b_parts]
    turned_spec = pl.BlockSpec((depth, n_out), lambda k: (k, 0))
    whole = pl.BlockSpec(shape, lambda k: (0, 0))
    out_shape, out_specs = jax.ShapeDtypeStruct(shape, jnp.float32), whole
    if sums is None:
        store_specs = [
            pl.BlockSpec((n_out, depth), lambda k: (0, k)),
            pl.BlockSpec((n_out, depth), lambda k: (0, k + steps)),
        ]
        turned = jax.ShapeDtypeStruct((half, n_out), stores[0].dtype)
        out_shape, out_specs = (out_shape, turned, turned), (whole, turned_spec, turned_spec)
        earlier = []
    else:
        store_specs = [turned_spec] * 2
        earlier = [sums]
    return pl.pallas_call(
        functools.partial(add_kernel, offsets, len(a_parts) // len(offsets)),
        grid=(steps,),
        out_shape=out_shape,
        in_specs=part_specs + store_specs + [whole] * len(earlier),
        out_specs=out_specs,
        compiler_params=pltpu.CompilerParams(vmem_limit_bytes=26 * 1024 * 1024),
        cost_estimate=pl.CostEstimate(
            flops=4 * n_rows * half * n_out,
            bytes_accessed=4 * half * (n_out + n_rows),
            transcendentals=0,
        ),
    )(*a_parts, *b_parts, *stores, *earlier)


def add_last(sums, offset, a_parts, b_parts, turned, depth):
    flat = lambda v: v.reshape(-1, v.shape[-1])
    operands = [flat(v) for v in (*a_parts, *b_parts)] + [*turned, sums]
    vmem = pl.BlockSpec(memory_space=pltpu.VMEM)
    return pl.pallas_call(
        functools.partial(last_kernel, offset, depth),
        out_shape=jax.ShapeDtypeStruct(sums.shape, sums.dtype),
        in_specs=[vmem] * len(operands),
        out_specs=vmem,
        input_output_aliases={len(operands) - 1: 0},
        compiler_params=pltpu.CompilerParams(vmem_limit_bytes=26 * 1024 * 1024),
    )(*operands)


def finish_kernel(order, mine, other, weight, out, scaled):
    n_out = out.shape[1]
    for i in range(0, out.shape[0], 128):
        rows = slice(i, i + 128)
        both = mine[rows, :] + other[rows, :]
        norm = jnp.sum(both[:, n_out:], axis=1, keepdims=True)
        scaled[rows, :] = both[:, :n_out] * weight[...] * lax.rsqrt(norm + 1e-06)
    for i in range(0, out.shape[0], 16):
        pair = [scaled[pl.ds(pl.multiple_of(order[i // 8 + j] * 8, 8), 8), :] for j in range(2)]
        out[i : i + 16, :] = jnp.concatenate(pair, 0).astype(out.dtype)


def absolute_order(zh, x, y):
    r = jnp.arange(RING, dtype=jnp.int32)

    def place(at):
        off = (r - at) % RING
        return jnp.where(off == 0, 0, jnp.where(off == 3, 1, off + 1))

    pz, px, py = place(zh), place(x), place(y)
    return (py[None, None, :] * 16 + px[None, :, None] * 4 + pz[:, None, None]).reshape(-1)


def per_device(queries, train_feats, train_weight):
    own = queries[0, :, 0, :][None]
    store = train_feats[:, 0, :]
    half = own.shape[-1] // 2
    a_planes, b_planes = (
        jnp.concatenate(v, 0) for v in z_planes(own[..., :half], own[..., half:])
    )
    first = jnp.concatenate(ring(a_planes, "x"), 0)
    second = jnp.concatenate(ring(b_planes, "y"), 0)
    a, b = ring(first, "y"), ring(second, "x")
    n_out = store.shape[0]
    sums, *turned = add_blocks(None, (0,), a[:1], b[:1], (store, store), n_out, 2048)
    sums = add_blocks(sums, (1, 2), a[1:3], b[1:3], turned, n_out, 2048)
    sums = add_last(sums, 3, a[3:], b[3:], turned, 2048)
    other = shift(sums, "layer", 1)
    order = absolute_order(*(lax.axis_index(n) for n in ("zh", "x", "y")))
    vmem = pl.BlockSpec(memory_space=pltpu.VMEM)
    result = pl.pallas_call(
        finish_kernel,
        out_shape=jax.ShapeDtypeStruct((sums.shape[0], n_out), jnp.bfloat16),
        in_specs=[pl.BlockSpec(memory_space=pltpu.SMEM)] + [vmem] * 3,
        out_specs=vmem,
        scratch_shapes=[pltpu.VMEM((sums.shape[0], n_out), jnp.float32)],
        compiler_params=pltpu.CompilerParams(vmem_limit_bytes=16 * 1024 * 1024),
    )(order, sums, other, train_weight[None, :])
    return result[None, :, :]


def solution(mesh):
    fine = Mesh(
        mesh.devices.reshape(RING, RING, RING, mesh.shape["layer"], mesh.shape["query"]),
        ("zh", "x", "y", "layer", "query"),
    )
    train = ("zh", "x", "y")
    return jax.shard_map(
        per_device,
        mesh=fine,
        in_specs=(P("query", train, "layer", None), P(train, "layer", None), P(train)),
        out_specs=P("query", None, train),
        check_vma=False,
    )
```
